32 devices in a mesh: dp: 16 (over z, y, core), tensor: 2 (over x).
Axes of the slice: x: 2, y: 2, z: 4, core: 2. Of those that a mesh axis runs over, the one named last changes fastest.
Arguments:
- tokens: bfloat16 [65536, 1024], P(('dp', 'tensor')), may hold values from -6 to 6
- lengths: int32 [16, 8], P('dp'), may hold values from 1 to 512, as said below
- cotangent: bfloat16 [65536, 1024], P(('dp', 'tensor')), may hold values from -6 to 6
- query_weight: bfloat16 [1024, 1024], P(None, 'tensor'), may hold values from -0.1875 to 0.1875
- query_bias: bfloat16 [1024], P('tensor'), may hold values from -3 to 3
- key_weight: bfloat16 [1024, 1024], P(None, 'tensor'), may hold values from -0.1875 to 0.1875
- value_weight: bfloat16 [1024, 1024], P(None, 'tensor'), may hold values from -0.1875 to 0.1875
- value_bias: bfloat16 [1024], P('tensor'), may hold values from -3 to 3
- out_weight: bfloat16 [1024, 1024], P('tensor'), may hold values from -0.75 to 0.75
- out_bias: bfloat16 [1024], replicated, may hold values from -3 to 3
- first_gain: float32 [1024], replicated, may hold values from 0.1 to 1.9
- first_shift: float32 [1024], replicated, may hold values from -3 to 3
- up_weight: bfloat16 [1024, 4096], P(None, 'tensor'), may hold values from -0.1875 to 0.1875
- up_bias: bfloat16 [4096], P('tensor'), may hold values from -3 to 3
- down_weight: bfloat16 [4096, 1024], P('tensor'), may hold values from -0.09375 to 0.09375
- down_bias: bfloat16 [1024], replicated, may hold values from -3 to 3
- second_gain: float32 [1024], replicated, may hold values from 0.1 to 1.9
- second_shift: float32 [1024], replicated, may hold values from -3 to 3
Outputs:
- layer_out: float32 [65536, 1024], P(('dp', 'tensor'))
- grad_tokens: float32 [65536, 1024], P(('dp', 'tensor'))
- wgrad_query: float32 [1024, 1024], P(None, 'tensor')
- bgrad_query: float32 [1024], P('tensor')
- wgrad_key: float32 [1024, 1024], P(None, 'tensor')
- wgrad_value: float32 [1024, 1024], P(None, 'tensor')
- bgrad_value: float32 [1024], P('tensor')
- wgrad_out: float32 [1024, 1024], P('tensor')
- bgrad_out: float32 [1024], replicated
- ggrad_first: float32 [1024], replicated
- sgrad_first: float32 [1024], replicated
- wgrad_up: float32 [1024, 4096], P(None, 'tensor')
- bgrad_up: float32 [4096], P('tensor')
- wgrad_down: float32 [4096, 1024], P('tensor')
- bgrad_down: float32 [1024], replicated
- ggrad_second: float32 [1024], replicated
- sgrad_second: float32 [1024], replicated
The draws below stay inside these ranges and needn't reach their ends.
Inputs may be any that keep to these rules, and one draw needn't show every extreme that they name: `lengths`: every group has at least one slot of length 512.
All inputs are finite; a program needn't handle non-finite values.
Results may differ from the reference program's by a relative error of at most 0.02.
Values may be sent and summed in bfloat16 or wider, within the bound.
A program may use at most 320 MiB of HBM per device.

```python
import jax
import jax.numpy as jnp
from jax import lax

D = 1024
HEADS = 16
HEAD_DIM = 64
FF = 4096
SEQ_LEN = 512
SEQS = 8
TOKENS = 65536
N_DP = 16


def draw_lengths(key, part):
    key = jax.random.fold_in(key, 11)
    first_key, second_key, third_key = jax.random.split(key, 3)
    ceiling = jax.random.randint(first_key, (N_DP, 1), SEQ_LEN // 2, SEQ_LEN + 1)
    raw_bits = jax.random.randint(second_key, (N_DP, SEQS), 0, 1 << 20)
    floor_part = ceiling // 2
    drawn = floor_part + raw_bits % (ceiling - floor_part + 1)
    full_slot = jax.random.randint(third_key, (N_DP, 1), 0, SEQS)
    slot_ids = jnp.arange(SEQS, dtype=jnp.int32)[None, :]
    drawn = jnp.where(slot_ids == full_slot, SEQ_LEN, drawn)
    return jnp.maximum(drawn, 1).astype(jnp.int32)


def block_levels(own_key, extent, pieces, low, high):
    level, own = 1.0, jax.random.fold_in(own_key, 6)
    for position, shards_of in pieces:
        draws = jnp.exp(jax.random.uniform(jax.random.fold_in(own, position), (shards_of,), jnp.float32, low / len(pieces), high / len(pieces)))
        level = level * jnp.repeat(draws, extent[position] // shards_of).reshape([-1 if axis == position else 1 for axis in range(len(extent))])
    return level


def scatter_about(rng, shape, scale, bound, pieces=(), kind=jnp.bfloat16):
    entries = scale * jax.random.normal(rng, shape, jnp.float32)
    if pieces:
        entries = entries * block_levels(rng, shape, pieces, -0.22, 0.18)
    return jnp.clip(entries, -bound, bound).astype(kind)


def setup_inputs(seed: int = 0) -> dict:
    key_of = jax.random.split(jax.random.key(seed), 19)
    return {
        "tokens": scatter_about(key_of[0], (TOKENS, D), 1.0, 6.0, ((0, 32),)),
        "lengths": draw_lengths(jax.random.fold_in(key_of[18], 71), 0),
        "cotangent": scatter_about(key_of[2], (TOKENS, D), 1.0, 6.0, ((0, 32),)),
        "query_weight": scatter_about(key_of[3], (D, D), D ** -0.5, 0.1875, ((1, 2),)),
        "query_bias": scatter_about(key_of[4], (D,), 0.5, 3.0, ((0, 2),)),
        "key_weight": scatter_about(key_of[5], (D, D), D ** -0.5, 0.1875, ((1, 2),)),
        "value_weight": scatter_about(key_of[6], (D, D), D ** -0.5, 0.1875, ((1, 2),)),
        "value_bias": scatter_about(key_of[7], (D,), 0.5, 3.0, ((0, 2),)),
        "out_weight": scatter_about(key_of[8], (D, D), (D // 16) ** -0.5, 0.75, ((0, 2),)),
        "out_bias": scatter_about(key_of[9], (D,), 0.5, 3.0),
        "first_gain": jnp.clip(1.0 + 0.18 * jax.random.normal(key_of[10], (D,), jnp.float32), 0.1, 1.9),
        "first_shift": scatter_about(key_of[11], (D,), 0.5, 3.0, (), jnp.float32),
        "up_weight": scatter_about(key_of[12], (D, FF), D ** -0.5, 0.1875, ((1, 2),)),
        "up_bias": scatter_about(key_of[13], (FF,), 0.5, 3.0, ((0, 2),)),
        "down_weight": scatter_about(key_of[14], (FF, D), FF ** -0.5, 0.09375, ((0, 2),)),
        "down_bias": scatter_about(key_of[15], (D,), 0.5, 3.0),
        "second_gain": jnp.clip(1.0 + 0.18 * jax.random.normal(key_of[16], (D,), jnp.float32), 0.1, 1.9),
        "second_shift": scatter_about(key_of[17], (D,), 0.5, 3.0, (), jnp.float32),
    }


@jax.custom_vjp
def low(v):
    return lax.optimization_barrier(v.astype(jnp.bfloat16)).astype(jnp.float32)

@jax.custom_vjp
def low_back(v):
    return v

def low_keep(v):
    return (low(v), None)

def low_pass(kept, grad):
    return (grad,)

def back_keep(v):
    return (v, None)

def back_low(kept, grad):
    return (low(grad),)
low.defvjp(low_keep, low_pass)
low_back.defvjp(back_keep, back_low)
highest = lax.Precision.HIGHEST
epsilon = 1e-12

def matmul(left, right):
    return jnp.dot(left, right, preferred_element_type=jnp.float32, precision=highest)

def normalize(summed, gain, shift):
    middle = lax.optimization_barrier(jnp.mean(summed, axis=-1, keepdims=True))
    centred = summed - middle
    spread = lax.optimization_barrier(jnp.mean(centred * centred, axis=-1, keepdims=True))
    return centred * lax.rsqrt(spread + epsilon) * gain + shift

def attend(block):
    queries, key_rows, value_rows, valid_keys = block
    scores = jnp.einsum('qhe,khe->hqk', queries, key_rows, precision=highest) * HEAD_DIM ** (-0.5)
    scores = jnp.where(valid_keys[None, None, :], low_back(scores), -1e+30)
    attn_probs = jax.nn.softmax(scores, axis=-1)
    return jnp.einsum('hqk,khe->qhe', low(attn_probs), value_rows, precision=highest)

def forward(params, tokens_rows, lengths_row):
    query_weight, query_bias, key_weight, value_weight, value_bias, out_weight, out_bias, first_gain, first_shift, up_weight, up_bias, down_weight, down_bias, second_gain, second_shift = params
    group_rows = tokens_rows.shape[0]
    queries = low(low_back(matmul(tokens_rows, query_weight)) + query_bias)
    key_rows = low(low_back(matmul(tokens_rows, key_weight)))
    value_rows = low(low_back(matmul(tokens_rows, value_weight)) + value_bias)
    valid_keys = jnp.arange(SEQ_LEN)[None, :] < lengths_row[:, None]
    mixed = lax.map(jax.checkpoint(attend), (queries.reshape(SEQS, SEQ_LEN, HEADS, HEAD_DIM), key_rows.reshape(SEQS, SEQ_LEN, HEADS, HEAD_DIM), value_rows.reshape(SEQS, SEQ_LEN, HEADS, HEAD_DIM), valid_keys))
    mixed = low(low_back(mixed.reshape(group_rows, D)))
    first_sum = tokens_rows + low_back(matmul(mixed, out_weight)) + out_bias
    hidden = normalize(first_sum, first_gain, first_shift)
    inner = low_back(matmul(low(hidden), up_weight)) + up_bias
    active = low(jax.nn.gelu(inner, approximate=False))
    second_sum = hidden + low_back(matmul(active, down_weight)) + down_bias
    return normalize(second_sum, second_gain, second_shift)

def reference(tokens, lengths, cotangent, query_weight, query_bias, key_weight, value_weight, value_bias, out_weight, out_bias, first_gain, first_shift, up_weight, up_bias, down_weight, down_bias, second_gain, second_shift):
    params = tuple((item.astype(jnp.float32) for item in (query_weight, query_bias, key_weight, value_weight, value_bias, out_weight, out_bias, first_gain, first_shift, up_weight, up_bias, down_weight, down_bias, second_gain, second_shift)))
    group_rows = SEQS * SEQ_LEN
    tokens_groups = tokens.astype(jnp.float32).reshape(N_DP, group_rows, D)
    cot_groups = cotangent.astype(jnp.float32).reshape(N_DP, group_rows, D)

    def one_group(totals, inputs):
        tokens_rows, cot_rows, lengths_row = inputs
        row_ids = jnp.arange(group_rows)
        row_live = row_ids % SEQ_LEN < lengths_row[row_ids // SEQ_LEN]
        outputs, pullback = jax.vjp(lambda pp, tt: forward(pp, tt, lengths_row), params, tokens_rows)
        grads_params, grads_rows = pullback(cot_rows * row_live[:, None].astype(jnp.float32))
        totals = jax.tree.map(lambda first, second: first + second, totals, grads_params)
        return (totals, (outputs, grads_rows))
    zeros = jax.tree.map(jnp.zeros_like, params)
    totals, (outputs, grads_rows) = lax.scan(one_group, zeros, (tokens_groups, cot_groups, lengths))
    return (outputs.reshape(TOKENS, D), grads_rows.reshape(TOKENS, D), totals[0], totals[1], totals[2], totals[3], totals[4], totals[5], totals[6], totals[7], totals[8], totals[9], totals[10], totals[11], totals[12], totals[13], totals[14])
```

```python
import jax
import jax.numpy as jnp
from jax import lax
from jax.experimental import pallas as pl
from jax.experimental.pallas import tpu as pltpu
from jax.sharding import PartitionSpec as P

HEAD_DIM = 64
SEQ_LEN = 512
LANES = 128
SCALE = HEAD_DIM ** (-0.5)


epsilon = 1e-12
low = jnp.bfloat16
wide = jnp.float32


def contract_rows(left, right):
    return lax.dot_general(left, right, (((0,), (0,)), ((), ())), preferred_element_type=wide)


def contract_cols(left, right):
    return lax.dot_general(left, right, (((1,), (1,)), ((), ())), preferred_element_type=wide)


def matmul(left, right):
    return jnp.dot(left, right, preferred_element_type=wide)


def center(summed):
    middle = jnp.mean(summed, axis=-1, keepdims=True)
    centred = summed - middle
    spread = jnp.mean(centred * centred, axis=-1, keepdims=True)
    scale = lax.rsqrt(spread + epsilon)
    return centred * scale, scale


def center_back(normed, scale, gain, grad):
    scaled = gain * grad
    mean_scaled = jnp.mean(scaled, axis=-1, keepdims=True)
    mean_both = jnp.mean(scaled * normed, axis=-1, keepdims=True)
    return (scaled - mean_scaled - normed * mean_both) * scale


def head_masks():
    column = lax.broadcasted_iota(jnp.int32, (1, LANES), 1)
    return [
        (column // HEAD_DIM == head).astype(wide).astype(low) for head in range(LANES // HEAD_DIM)
    ]


def attend_kernel(lengths_ref, query_ref, key_ref, value_ref, mixed_ref):
    length = lengths_ref[pl.program_id(1)]
    key_id = lax.broadcasted_iota(jnp.int32, (1, SEQ_LEN), 1)
    shut = jnp.where(key_id < length, 0.0, -1e30)
    queries = query_ref[...] * jnp.asarray(SCALE, low)
    keys = key_ref[...]
    values = value_ref[...]
    mixed = None
    for mask in head_masks():
        scores = contract_cols(queries * mask, keys) + shut
        raised = jnp.exp(scores - jnp.max(scores, axis=-1, keepdims=True))
        total = jnp.sum(raised, axis=-1, keepdims=True)
        part = matmul(raised.astype(low), values * mask) * (1.0 / total)
        mixed = part if mixed is None else mixed + part
    mixed_ref[...] = mixed.astype(low)


def attend_back_kernel(
    lengths_ref,
    query_ref,
    key_ref,
    value_ref,
    grad_ref,
    grad_query_ref,
    grad_key_ref,
    grad_value_ref,
    query_sum_ref,
    value_sum_ref,
):
    length = lengths_ref[pl.program_id(1)]
    key_id = lax.broadcasted_iota(jnp.int32, (SEQ_LEN, 1), 0)
    shut = jnp.where(key_id < length, 0.0, -1e30)
    queries = query_ref[...] * jnp.asarray(SCALE, low)
    keys = key_ref[...]
    keys_scaled = keys * jnp.asarray(SCALE, low)
    values = value_ref[...]
    grads = grad_ref[...]
    grad_query = grad_key = grad_value = 0.0
    for mask in head_masks():
        head_queries = queries * mask
        head_grads = grads * mask
        scores = contract_cols(keys, head_queries) + shut
        raised = jnp.exp(scores - jnp.max(scores, axis=0, keepdims=True))
        probs = raised * (1.0 / jnp.sum(raised, axis=0, keepdims=True))
        grad_probs = contract_cols(values, head_grads)
        both = jnp.sum(grad_probs * probs, axis=0, keepdims=True)
        grad_scores = (probs * (grad_probs - both)).astype(low)
        grad_value += matmul(probs.astype(low), head_grads)
        grad_key += matmul(grad_scores, head_queries)
        grad_query += contract_rows(grad_scores, keys_scaled * mask)
    grad_query_ref[...] = grad_query.astype(low)
    grad_key_ref[...] = grad_key.astype(low)
    grad_value_ref[...] = grad_value.astype(low)

    @pl.when(pl.program_id(1) == 0)
    def _():
        query_sum_ref[...] = jnp.zeros_like(query_sum_ref)
        value_sum_ref[...] = jnp.zeros_like(value_sum_ref)

    query_sum_ref[...] += jnp.sum(grad_query, axis=0, keepdims=True)
    value_sum_ref[...] += jnp.sum(grad_value, axis=0, keepdims=True)


def block_specs():
    rows = pl.BlockSpec((SEQ_LEN, LANES), lambda j, i: (i, j))
    sums = pl.BlockSpec((1, LANES), lambda j, i: (0, j))
    return pl.BlockSpec(memory_space=pltpu.SMEM), rows, sums


def attend(lengths, queries, keys, values):
    rows, width = queries.shape
    scalars, block, _ = block_specs()
    pairs = rows * width * SEQ_LEN
    return pl.pallas_call(
        attend_kernel,
        grid=(width // LANES, rows // SEQ_LEN),
        in_specs=[scalars] + [block] * 3,
        out_specs=block,
        out_shape=jax.ShapeDtypeStruct((rows, width), low),
        compiler_params=pltpu.CompilerParams(vmem_limit_bytes=32 * 2**20),
        cost_estimate=pl.CostEstimate(
            flops=16 * pairs, bytes_accessed=8 * rows * width, transcendentals=pairs // HEAD_DIM
        ),
    )(lengths, queries, keys, values)


def attend_back(lengths, queries, keys, values, grads):
    rows, width = queries.shape
    scalars, block, sums = block_specs()
    pairs = rows * width * SEQ_LEN
    return pl.pallas_call(
        attend_back_kernel,
        grid=(width // LANES, rows // SEQ_LEN),
        in_specs=[scalars] + [block] * 4,
        out_specs=[block] * 3 + [sums] * 2,
        out_shape=[jax.ShapeDtypeStruct((rows, width), low)] * 3
        + [jax.ShapeDtypeStruct((1, width), wide)] * 2,
        compiler_params=pltpu.CompilerParams(vmem_limit_bytes=32 * 2**20),
        cost_estimate=pl.CostEstimate(
            flops=40 * pairs, bytes_accessed=14 * rows * width, transcendentals=pairs // HEAD_DIM
        ),
    )(lengths, queries, keys, values, grads)


def sharing(dp, tensor):
    if tensor == 2 and dp % 2 == 0:
        over = [(0, 1), (1, 0)]
        mates = [(i, i ^ 1) for i in range(dp)]
        lane = lambda: lax.axis_index("dp") % 2

        def spread(weight, axis):
            half = weight.shape[axis] // 2
            mine = lax.dynamic_slice_in_dim(weight, lane() * half, half, axis)
            fetched = lax.ppermute(mine, "tensor", over)
            passed = lax.ppermute(fetched, "dp", mates)
            return [weight, jnp.concatenate([fetched, passed], axis=axis)]

        def spread_vector(vector):
            half = vector.shape[0] // 2
            other = lax.ppermute(vector, "tensor", over)
            return [vector, jnp.where(lane() == 0, other, jnp.roll(other, half))]

        def collect(grads, axis):
            own, other = grads
            half = other.shape[axis] // 2
            first, last = jnp.split(other, 2, axis=axis)
            arrived = lax.ppermute(last.astype(low), "dp", mates)
            summed = (first + arrived.astype(wide)).astype(low)
            term = lax.ppermute(summed, "tensor", over).astype(wide)
            left, right = jnp.split(own, 2, axis=axis)
            return jnp.concatenate(
                [
                    (left + jnp.where(lane() == 0, term, 0.0)).astype(low),
                    (right + jnp.where(lane() == 1, term, 0.0)).astype(low),
                ],
                axis=axis,
            )

        def order(sums):
            own, other = sums
            half = other.shape[0] // 2
            other = jnp.where(lane() == 0, other, jnp.roll(other, half))
            whole = jnp.stack([own, other])
            return jnp.where(lax.axis_index("tensor") == 0, whole, whole[::-1]).reshape(-1)

    else:

        def spread(weight, axis):
            return [lax.all_gather(weight, "tensor", axis=axis, tiled=True)]

        def spread_vector(vector):
            return [lax.all_gather(vector, "tensor", axis=0, tiled=True)]

        def collect(grads, axis):
            return lax.psum_scatter(
                grads[0].astype(low), "tensor", scatter_dimension=axis, tiled=True
            )

        def order(sums):
            return sums[0]

    return spread, spread_vector, collect, order


def make_shards(dp, tensor):
    spread, spread_vector, collect, order = sharing(dp, tensor)

    def shards(
        tokens,
        lengths,
        cotangent,
        query_weight,
        query_bias,
        key_weight,
        value_weight,
        value_bias,
        out_weight,
        out_bias,
        first_gain,
        first_shift,
        up_weight,
        up_bias,
        down_weight,
        down_bias,
        second_gain,
        second_shift,
    ):
        rows = tokens.shape[0]
        slots = rows // SEQ_LEN
        place = lax.axis_index("tensor")
        my_lengths = lax.dynamic_slice_in_dim(lengths[0], place * slots, slots, 0)
        row_live = (
            jnp.arange(SEQ_LEN, dtype=jnp.int32)[None, :] < my_lengths[:, None]
        ).astype(wide).reshape(rows, 1)

        query_parts = spread(query_weight, 1)
        key_parts = spread(key_weight, 1)
        value_parts = spread(value_weight, 1)
        out_parts = spread(out_weight, 0)
        up_parts = spread(up_weight, 1)
        down_parts = spread(down_weight, 0)
        query_biases = spread_vector(query_bias)
        value_biases = spread_vector(value_bias)
        up_biases = spread_vector(up_bias)
        pieces = range(len(query_parts))

        attended = []
        attn_sum = 0.0
        for i in pieces:
            queries = (matmul(tokens, query_parts[i]) + query_biases[i].astype(wide)).astype(low)
            keys = matmul(tokens, key_parts[i]).astype(low)
            values = (matmul(tokens, value_parts[i]) + value_biases[i].astype(wide)).astype(low)
            mixed = attend(my_lengths, queries, keys, values)
            attended.append((queries, keys, values, mixed))
            attn_sum += matmul(mixed, out_parts[i])
        first_sum = tokens.astype(wide) + attn_sum + out_bias.astype(wide)
        first_normed, first_scale = center(first_sum)
        hidden = first_normed * first_gain + first_shift
        hidden_low = hidden.astype(low)

        branch = 0.0
        inner_parts = []
        for i in pieces:
            inner = matmul(hidden_low, up_parts[i]) + up_biases[i].astype(wide)
            phi = 0.5 + 0.5 * lax.erf(inner * 0.5**0.5)
            slope = phi + inner * (jnp.exp(inner * inner * -0.5) * 0.3989422804014327)
            active = (inner * phi).astype(low)
            inner_parts.append((active, slope.astype(low)))
            branch += matmul(active, down_parts[i])
        second_sum = hidden + branch + down_bias.astype(wide)
        second_normed, second_scale = center(second_sum)
        layer_out = second_normed * second_gain + second_shift

        grad_out = cotangent.astype(wide) * row_live
        grad_second = center_back(second_normed, second_scale, second_gain, grad_out)
        ggrad_second = jnp.sum(grad_out * second_normed, axis=0)
        sgrad_second = jnp.sum(grad_out, axis=0)
        bgrad_down = jnp.sum(grad_second, axis=0)
        grad_second_low = grad_second.astype(low)

        grads_down, grads_up, sums_up = [None] * 2, [None] * 2, [None] * 2
        back_hidden = 0.0
        for i in reversed(pieces):
            active, slope = inner_parts[i]
            grads_down[i] = contract_rows(active, grad_second_low)
            grad_inner = contract_cols(grad_second_low, down_parts[i]) * slope.astype(wide)
            sums_up[i] = jnp.sum(grad_inner, axis=0)
            grad_inner = grad_inner.astype(low)
            grads_up[i] = contract_rows(hidden_low, grad_inner)
            back_hidden += contract_cols(grad_inner, up_parts[i])
        wgrad_down = collect(grads_down, 0)
        wgrad_up = collect(grads_up, 1)
        wgrad_down = lax.psum(wgrad_down, "dp")

        grad_hidden = grad_second + back_hidden
        grad_first = center_back(first_normed, first_scale, first_gain, grad_hidden)
        ggrad_first = jnp.sum(grad_hidden * first_normed, axis=0)
        sgrad_first = jnp.sum(grad_hidden, axis=0)
        bgrad_out = jnp.sum(grad_first, axis=0)
        grad_first_low = grad_first.astype(low)

        grads_out, grads_query, grads_key, grads_value = ([None] * 2 for _ in range(4))
        sums_query, sums_value = [None] * 2, [None] * 2
        grad_tokens = grad_first
        for i in reversed(pieces):
            queries, keys, values, mixed = attended[i]
            grads_out[i] = contract_rows(mixed, grad_first_low)
            grad_mixed = contract_cols(grad_first_low, out_parts[i]).astype(low)
            grad_query, grad_key, grad_value, query_sum, value_sum = attend_back(
                my_lengths, queries, keys, values, grad_mixed
            )
            sums_query[i] = query_sum[0]
            sums_value[i] = value_sum[0]
            grads_query[i] = contract_rows(tokens, grad_query)
            grads_key[i] = contract_rows(tokens, grad_key)
            grads_value[i] = contract_rows(tokens, grad_value)
            grad_tokens += (
                contract_cols(grad_query, query_parts[i])
                + contract_cols(grad_key, key_parts[i])
                + contract_cols(grad_value, value_parts[i])
            )
        wgrad_out = collect(grads_out, 0)
        wgrad_up, wgrad_out, wgrad_down = lax.optimization_barrier(
            (wgrad_up, wgrad_out, wgrad_down)
        )
        wgrad_up, wgrad_out = lax.psum((wgrad_up, wgrad_out), "dp")
        last = [collect(grads, 1) for grads in (grads_query, grads_key, grads_value)]
        *last, wgrad_up, wgrad_out = lax.optimization_barrier((*last, wgrad_up, wgrad_out))
        wgrad_query, wgrad_key, wgrad_value = lax.psum(tuple(last), "dp")

        vectors = [order(sums) for sums in (sums_query, sums_value, sums_up)]
        vectors += [
            bgrad_out,
            ggrad_first,
            sgrad_first,
            bgrad_down,
            ggrad_second,
            sgrad_second,
        ]
        edges, size = [], 0
        for vector in vectors[:-1]:
            size += vector.shape[0]
            edges.append(size)
        vectors = jnp.split(lax.psum(jnp.concatenate(vectors), ("dp", "tensor")), edges)
        for i in range(3):
            share = vectors[i].shape[0] // tensor
            vectors[i] = lax.dynamic_slice_in_dim(vectors[i], place * share, share, 0)
        (
            bgrad_query,
            bgrad_value,
            bgrad_up,
            bgrad_out,
            ggrad_first,
            sgrad_first,
            bgrad_down,
            ggrad_second,
            sgrad_second,
        ) = vectors
        return (
            layer_out,
            grad_tokens,
            wgrad_query.astype(wide),
            bgrad_query,
            wgrad_key.astype(wide),
            wgrad_value.astype(wide),
            bgrad_value,
            wgrad_out.astype(wide),
            bgrad_out,
            ggrad_first,
            sgrad_first,
            wgrad_up.astype(wide),
            bgrad_up,
            wgrad_down.astype(wide),
            bgrad_down,
            ggrad_second,
            sgrad_second,
        )

    return shards


def solution(mesh):
    return jax.shard_map(
        make_shards(mesh.shape["dp"], mesh.shape["tensor"]),
        mesh=mesh,
        in_specs=(
            P(("dp", "tensor"), None),
            P("dp", None),
            P(("dp", "tensor"), None),
            P(None, "tensor"),
            P("tensor"),
            P(None, "tensor"),
            P(None, "tensor"),
            P("tensor"),
            P("tensor", None),
            P(),
            P(),
            P(),
            P(None, "tensor"),
            P("tensor"),
            P("tensor", None),
            P(),
            P(),
            P(),
        ),
        out_specs=(
            P(("dp", "tensor"), None),
            P(("dp", "tensor"), None),
            P(None, "tensor"),
            P("tensor"),
            P(None, "tensor"),
            P(None, "tensor"),
            P("tensor"),
            P("tensor", None),
            P(),
            P(),
            P(),
            P(None, "tensor"),
            P("tensor"),
            P("tensor", None),
            P(),
            P(),
            P(),
        ),
        check_vma=False,
    )
```

```python
import jax
import jax.numpy as jnp
from jax import lax
from jax.experimental import pallas as pl
from jax.experimental.pallas import tpu as pltpu
from jax.sharding import PartitionSpec as P

HEAD_DIM = 64
SEQ_LEN = 512
LANES = 128
SCALE = HEAD_DIM ** (-0.5)


epsilon = 1e-12
low = jnp.bfloat16
wide = jnp.float32


def contract_rows(left, right):
    return lax.dot_general(left, right, (((0,), (0,)), ((), ())), preferred_element_type=wide)


def contract_cols(left, right):
    return lax.dot_general(left, right, (((1,), (1,)), ((), ())), preferred_element_type=wide)


hold = lax.optimization_barrier


def matmul(left, right):
    return jnp.dot(left, right, preferred_element_type=wide)


def center(summed):
    middle = jnp.mean(summed, axis=-1, keepdims=True)
    centred = summed - middle
    spread = jnp.mean(centred * centred, axis=-1, keepdims=True)
    scale = lax.rsqrt(spread + epsilon)
    return centred * scale, scale


def center_back(normed, scale, gain, grad):
    scaled = gain * grad
    mean_scaled = jnp.mean(scaled, axis=-1, keepdims=True)
    mean_both = jnp.mean(scaled * normed, axis=-1, keepdims=True)
    return (scaled - mean_scaled - normed * mean_both) * scale


def head_masks():
    column = lax.broadcasted_iota(jnp.int32, (1, LANES), 1)
    return [
        (column // HEAD_DIM == head).astype(wide).astype(low) for head in range(LANES // HEAD_DIM)
    ]


def attend_kernel(lengths_ref, query_ref, key_ref, value_ref, mixed_ref):
    length = lengths_ref[pl.program_id(1)]
    key_id = lax.broadcasted_iota(jnp.int32, (1, SEQ_LEN), 1)
    shut = jnp.where(key_id < length, 0.0, -1e30)
    queries = query_ref[...] * jnp.asarray(SCALE, low)
    keys = key_ref[...]
    values = value_ref[...]
    mixed = None
    for mask in head_masks():
        scores = contract_cols(queries * mask, keys) + shut
        raised = jnp.exp(scores - jnp.max(scores, axis=-1, keepdims=True))
        total = jnp.sum(raised, axis=-1, keepdims=True)
        part = matmul(raised.astype(low), values * mask) * (1.0 / total)
        mixed = part if mixed is None else mixed + part
    mixed_ref[...] = mixed.astype(low)


def attend_back_kernel(
    lengths_ref,
    query_ref,
    key_ref,
    value_ref,
    grad_ref,
    grad_query_ref,
    grad_key_ref,
    grad_value_ref,
    query_sum_ref,
    value_sum_ref,
):
    length = lengths_ref[pl.program_id(1)]
    key_id = lax.broadcasted_iota(jnp.int32, (SEQ_LEN, 1), 0)
    shut = jnp.where(key_id < length, 0.0, -1e30)
    queries = query_ref[...] * jnp.asarray(SCALE, low)
    keys = key_ref[...]
    keys_scaled = keys * jnp.asarray(SCALE, low)
    values = value_ref[...]
    grads = grad_ref[...]
    grad_query = grad_key = grad_value = 0.0
    for mask in head_masks():
        head_queries = queries * mask
        head_grads = grads * mask
        scores = contract_cols(keys, head_queries) + shut
        raised = jnp.exp(scores - jnp.max(scores, axis=0, keepdims=True))
        probs = raised * (1.0 / jnp.sum(raised, axis=0, keepdims=True))
        grad_probs = contract_cols(values, head_grads)
        both = jnp.sum(grad_probs * probs, axis=0, keepdims=True)
        grad_scores = (probs * (grad_probs - both)).astype(low)
        grad_value += matmul(probs.astype(low), head_grads)
        grad_key += matmul(grad_scores, head_queries)
        grad_query += contract_rows(grad_scores, keys_scaled * mask)
    grad_query_ref[...] = grad_query.astype(low)
    grad_key_ref[...] = grad_key.astype(low)
    grad_value_ref[...] = grad_value.astype(low)

    @pl.when(pl.program_id(1) == 0)
    def _():
        query_sum_ref[...] = jnp.zeros_like(query_sum_ref)
        value_sum_ref[...] = jnp.zeros_like(value_sum_ref)

    query_sum_ref[...] += jnp.sum(grad_query, axis=0, keepdims=True)
    value_sum_ref[...] += jnp.sum(grad_value, axis=0, keepdims=True)


def block_specs():
    rows = pl.BlockSpec((SEQ_LEN, LANES), lambda j, i: (i, j))
    sums = pl.BlockSpec((1, LANES), lambda j, i: (0, j))
    return pl.BlockSpec(memory_space=pltpu.SMEM), rows, sums


def attend(lengths, queries, keys, values):
    rows, width = queries.shape
    scalars, block, _ = block_specs()
    pairs = rows * width * SEQ_LEN
    return pl.pallas_call(
        attend_kernel,
        grid=(width // LANES, rows // SEQ_LEN),
        in_specs=[scalars] + [block] * 3,
        out_specs=block,
        out_shape=jax.ShapeDtypeStruct((rows, width), low),
        compiler_params=pltpu.CompilerParams(vmem_limit_bytes=32 * 2**20),
        cost_estimate=pl.CostEstimate(
            flops=16 * pairs, bytes_accessed=8 * rows * width, transcendentals=pairs // HEAD_DIM
        ),
    )(lengths, queries, keys, values)


def attend_back(lengths, queries, keys, values, grads):
    rows, width = queries.shape
    scalars, block, sums = block_specs()
    pairs = rows * width * SEQ_LEN
    return pl.pallas_call(
        attend_back_kernel,
        grid=(width // LANES, rows // SEQ_LEN),
        in_specs=[scalars] + [block] * 4,
        out_specs=[block] * 3 + [sums] * 2,
        out_shape=[jax.ShapeDtypeStruct((rows, width), low)] * 3
        + [jax.ShapeDtypeStruct((1, width), wide)] * 2,
        compiler_params=pltpu.CompilerParams(vmem_limit_bytes=32 * 2**20),
        cost_estimate=pl.CostEstimate(
            flops=40 * pairs, bytes_accessed=14 * rows * width, transcendentals=pairs // HEAD_DIM
        ),
    )(lengths, queries, keys, values, grads)


def sharing(dp, tensor):
    if tensor == 2 and dp % 2 == 0:
        over = [(0, 1), (1, 0)]
        mates = [(i, i ^ 1) for i in range(dp)]
        lane = lambda: lax.axis_index("dp") % 2

        def spread(weight, axis):
            half = weight.shape[axis] // 2
            mine = lax.dynamic_slice_in_dim(weight, lane() * half, half, axis)
            fetched = lax.ppermute(mine, "tensor", over)
            passed = lax.ppermute(fetched, "dp", mates)
            return [weight, jnp.concatenate([fetched, passed], axis=axis)]

        def spread_vector(vector):
            half = vector.shape[0] // 2
            other = lax.ppermute(vector, "tensor", over)
            return [vector, jnp.where(lane() == 0, other, jnp.roll(other, half))]

        def pass_on(other, axis):
            return lax.ppermute(jnp.split(other, 2, axis=axis)[1], "dp", mates)

        def send_back(other, arrived, axis):
            first = jnp.split(other, 2, axis=axis)[0]
            summed = (first.astype(wide) + arrived.astype(wide)).astype(low)
            return lax.ppermute(summed, "tensor", over)

        def finish(own, term, axis):
            term = term.astype(wide)
            left, right = jnp.split(own, 2, axis=axis)
            return jnp.concatenate(
                [
                    (left + jnp.where(lane() == 0, term, 0.0)).astype(low),
                    (right + jnp.where(lane() == 1, term, 0.0)).astype(low),
                ],
                axis=axis,
            )

        def order(sums):
            own, other = sums
            half = other.shape[0] // 2
            other = jnp.where(lane() == 0, other, jnp.roll(other, half))
            whole = jnp.stack([own, other])
            return jnp.where(lax.axis_index("tensor") == 0, whole, whole[::-1]).reshape(-1)

    else:

        def spread(weight, axis):
            return [lax.all_gather(weight, "tensor", axis=axis, tiled=True)]

        def spread_vector(vector):
            return [lax.all_gather(vector, "tensor", axis=0, tiled=True)]

        def pass_on(other, axis):
            return None

        def send_back(other, arrived, axis):
            return None

        def finish(own, term, axis):
            return lax.psum_scatter(
                own.astype(low), "tensor", scatter_dimension=axis, tiled=True
            )

        def order(sums):
            return sums[0]

    return spread, spread_vector, pass_on, send_back, finish, order


def make_shards(dp, tensor):
    spread, spread_vector, pass_on, send_back, finish, order = sharing(dp, tensor)

    def shards(
        tokens,
        lengths,
        cotangent,
        query_weight,
        query_bias,
        key_weight,
        value_weight,
        value_bias,
        out_weight,
        out_bias,
        first_gain,
        first_shift,
        up_weight,
        up_bias,
        down_weight,
        down_bias,
        second_gain,
        second_shift,
    ):
        rows = tokens.shape[0]
        slots = rows // SEQ_LEN
        place = lax.axis_index("tensor")
        my_lengths = lax.dynamic_slice_in_dim(lengths[0], place * slots, slots, 0)
        row_live = (
            jnp.arange(SEQ_LEN, dtype=jnp.int32)[None, :] < my_lengths[:, None]
        ).astype(wide).reshape(rows, 1)

        query_parts = spread(query_weight, 1)
        key_parts = spread(key_weight, 1)
        value_parts = spread(value_weight, 1)
        out_parts = spread(out_weight, 0)
        up_parts = spread(up_weight, 1)
        down_parts = spread(down_weight, 0)
        query_biases = spread_vector(query_bias)
        value_biases = spread_vector(value_bias)
        up_biases = spread_vector(up_bias)
        pieces = range(len(query_parts))

        attended = []
        attn_sum = 0.0
        for i in pieces:
            queries = (matmul(tokens, query_parts[i]) + query_biases[i].astype(wide)).astype(low)
            keys = matmul(tokens, key_parts[i]).astype(low)
            values = (matmul(tokens, value_parts[i]) + value_biases[i].astype(wide)).astype(low)
            mixed = attend(my_lengths, queries, keys, values)
            attended.append((queries, keys, values, mixed))
            attn_sum += matmul(mixed, out_parts[i])
        first_sum = tokens.astype(wide) + attn_sum + out_bias.astype(wide)
        first_normed, first_scale = center(first_sum)
        hidden = first_normed * first_gain + first_shift
        hidden_low = hidden.astype(low)

        branch = 0.0
        inner_parts = []
        for i in pieces:
            inner = matmul(hidden_low, up_parts[i]) + up_biases[i].astype(wide)
            phi = 0.5 + 0.5 * lax.erf(inner * 0.5**0.5)
            slope = phi + inner * (jnp.exp(inner * inner * -0.5) * 0.3989422804014327)
            active = (inner * phi).astype(low)
            inner_parts.append((active, slope.astype(low)))
            branch += matmul(active, down_parts[i])
        second_sum = hidden + branch + down_bias.astype(wide)
        second_normed, second_scale = center(second_sum)
        layer_out = second_normed * second_gain + second_shift

        grad_out = cotangent.astype(wide) * row_live
        grad_second = center_back(second_normed, second_scale, second_gain, grad_out)
        ggrad_second = jnp.sum(grad_out * second_normed, axis=0)
        sgrad_second = jnp.sum(grad_out, axis=0)
        bgrad_down = jnp.sum(grad_second, axis=0)
        grad_second_low = grad_second.astype(low)

        grads_down, grads_up, sums_up = [None] * 2, [None] * 2, [None] * 2
        back_hidden = 0.0
        ffn_arrived = [None] * 2
        for i in reversed(pieces):
            active, slope = inner_parts[i]
            grads_down[i] = contract_rows(active, grad_second_low)
            grad_inner = contract_cols(grad_second_low, down_parts[i]) * slope.astype(wide)
            sums_up[i] = jnp.sum(grad_inner, axis=0)
            grad_inner = grad_inner.astype(low)
            grads_up[i] = contract_rows(hidden_low, grad_inner)
            back_hidden += contract_cols(grad_inner, up_parts[i])
            if i == 1:
                grads_down[1], grads_up[1] = grads_down[1].astype(low), grads_up[1].astype(low)
                grads_down[1], grads_up[1], grad_second_low = hold(
                    (grads_down[1], grads_up[1], grad_second_low)
                )
                ffn_arrived = [pass_on(grads_down[1], 0), pass_on(grads_up[1], 1)]
        back_hidden, ffn_arrived = hold((back_hidden, ffn_arrived))
        ffn_terms = [
            send_back(grads_down[1], ffn_arrived[0], 0),
            send_back(grads_up[1], ffn_arrived[1], 1),
        ]

        grad_hidden = grad_second + back_hidden
        grad_first = center_back(first_normed, first_scale, first_gain, grad_hidden)
        ggrad_first = jnp.sum(grad_hidden * first_normed, axis=0)
        sgrad_first = jnp.sum(grad_hidden, axis=0)
        bgrad_out = jnp.sum(grad_first, axis=0)
        grad_first_low = grad_first.astype(low)

        grads_out, grads_query, grads_key, grads_value = ([None] * 2 for _ in range(4))
        sums_query, sums_value = [None] * 2, [None] * 2
        grad_tokens = grad_first
        kinds = (grads_out, grads_query, grads_key, grads_value)
        axes = (0, 1, 1, 1)
        arrived = [None] * 4
        terms = [None] * 4
        for i in reversed(pieces):
            if i == 0:
                wgrad_down = finish(grads_down[0], ffn_terms[0], 0)
                wgrad_up = finish(grads_up[0], ffn_terms[1], 1)
                wgrad_down, wgrad_up, grad_first_low = hold(
                    (wgrad_down, wgrad_up, grad_first_low)
                )
                wgrad_down, wgrad_up = lax.psum((wgrad_down, wgrad_up), "dp")
            queries, keys, values, mixed = attended[i]
            grads_out[i] = contract_rows(mixed, grad_first_low)
            grad_mixed = contract_cols(grad_first_low, out_parts[i]).astype(low)
            grad_query, grad_key, grad_value, query_sum, value_sum = attend_back(
                my_lengths, queries, keys, values, grad_mixed
            )
            if i == 0:
                grad_query, grad_key, grad_value, arrived = hold(
                    (grad_query, grad_key, grad_value, arrived)
                )
                terms = [
                    send_back(grads[1], got, axis)
                    for grads, got, axis in zip(kinds, arrived, axes)
                ]
            sums_query[i] = query_sum[0]
            sums_value[i] = value_sum[0]
            grads_query[i] = contract_rows(tokens, grad_query)
            grads_key[i] = contract_rows(tokens, grad_key)
            grads_value[i] = contract_rows(tokens, grad_value)
            grad_tokens += (
                contract_cols(grad_query, query_parts[i])
                + contract_cols(grad_key, key_parts[i])
                + contract_cols(grad_value, value_parts[i])
            )
            if i == 1:
                for grads in kinds:
                    grads[1] = grads[1].astype(low)
                others, ffn_terms, grad_first_low = hold(
                    ([grads[1] for grads in kinds], ffn_terms, grad_first_low)
                )
                for grads, other in zip(kinds, others):
                    grads[1] = other
                arrived = [pass_on(other, axis) for other, axis in zip(others, axes)]
        last = [finish(grads[0], term, axis) for grads, term, axis in zip(kinds, terms, axes)]
        last, wgrad_down, wgrad_up = hold((last, wgrad_down, wgrad_up))
        wgrad_out, wgrad_query, wgrad_key, wgrad_value = lax.psum(tuple(last), "dp")

        vectors = [order(sums) for sums in (sums_query, sums_value, sums_up)]
        vectors += [
            bgrad_out,
            ggrad_first,
            sgrad_first,
            bgrad_down,
            ggrad_second,
            sgrad_second,
        ]
        edges, size = [], 0
        for vector in vectors[:-1]:
            size += vector.shape[0]
            edges.append(size)
        joined, _ = hold((jnp.concatenate(vectors), [grads[0] for grads in kinds]))
        vectors = jnp.split(lax.psum(joined, ("dp", "tensor")), edges)
        for i in range(3):
            share = vectors[i].shape[0] // tensor
            vectors[i] = lax.dynamic_slice_in_dim(vectors[i], place * share, share, 0)
        (
            bgrad_query,
            bgrad_value,
            bgrad_up,
            bgrad_out,
            ggrad_first,
            sgrad_first,
            bgrad_down,
            ggrad_second,
            sgrad_second,
        ) = vectors
        return (
            layer_out,
            grad_tokens,
            wgrad_query.astype(wide),
            bgrad_query,
            wgrad_key.astype(wide),
            wgrad_value.astype(wide),
            bgrad_value,
            wgrad_out.astype(wide),
            bgrad_out,
            ggrad_first,
            sgrad_first,
            wgrad_up.astype(wide),
            bgrad_up,
            wgrad_down.astype(wide),
            bgrad_down,
            ggrad_second,
            sgrad_second,
        )

    return shards


def solution(mesh):
    return jax.shard_map(
        make_shards(mesh.shape["dp"], mesh.shape["tensor"]),
        mesh=mesh,
        in_specs=(
            P(("dp", "tensor"), None),
            P("dp", None),
            P(("dp", "tensor"), None),
            P(None, "tensor"),
            P("tensor"),
            P(None, "tensor"),
            P(None, "tensor"),
            P("tensor"),
            P("tensor", None),
            P(),
            P(),
            P(),
            P(None, "tensor"),
            P("tensor"),
            P("tensor", None),
            P(),
            P(),
            P(),
        ),
        out_specs=(
            P(("dp", "tensor"), None),
            P(("dp", "tensor"), None),
            P(None, "tensor"),
            P("tensor"),
            P(None, "tensor"),
            P(None, "tensor"),
            P("tensor"),
            P("tensor", None),
            P(),
            P(),
            P(),
            P(None, "tensor"),
            P("tensor"),
            P("tensor", None),
            P(),
            P(),
            P(),
        ),
        check_vma=False,
    )
```
